128 devices in a mesh: tm: 16 (over x, y), panel: 8 (over z, core).
Axes of the slice: x: 4, y: 4, z: 4, core: 2. Of those that a mesh axis runs over, the one named last changes fastest.
Arguments:
- transitions: float32 [64, 512, 512], P('tm', 'panel'), may hold values from -1 to 1.1, as said below
- offsets: float32 [64, 512], P('tm', 'panel'), may hold values from -1.2 to 1.2
- noise_cov: float32 [64, 512, 512], P('tm', 'panel'), may hold values from -0.05 to 0.2, as said below
Outputs:
- smoothed_means: float32 [64, 512], P('tm', 'panel')
- smoothed_covs: float32 [64, 512, 512], P('tm', 'panel')
The draws below stay inside these ranges and needn't reach their ends.
Inputs may be any that keep to these rules, and one draw needn't show every extreme that they name: `transitions`: each row is a rate times a row of a near-identity matrix. `noise_cov`: symmetric.
All inputs are finite; a program needn't handle non-finite values.
Results may differ from the reference program's by a relative error of at most 0.00027.
Values sent between devices are 32-bit elements; how exact they have to be, the bound alone decides.
No kernel may reach another device: no remote copies, remote signals or barrier semaphores. Data moves between devices by JAX's collectives and lax.ppermute only.
A program may use at most 128 MiB of HBM per device.

```python
import math
import jax
import jax.numpy as jnp
from jax import lax

D = 512
EPOCH_COUNT_ALL = 64


def draw_transitions(key, part):
    key = jax.random.fold_in(key, 1)
    stochastic_seed_list = jax.random.split(key, 5)
    share = 0.5
    slow = jax.random.bernoulli(stochastic_seed_list[0], share, (D,))
    slow_rate = jax.random.uniform(stochastic_seed_list[1], (EPOCH_COUNT_ALL, D), jnp.float32, 0.975, 0.995)
    fast_rate = jax.random.uniform(stochastic_seed_list[2], (EPOCH_COUNT_ALL, D), jnp.float32, 0.3, 0.9)
    mean_wander_speeds = jnp.where(slow[None, :], slow_rate, fast_rate)
    draw_batch_group = jax.random.bernoulli(stochastic_seed_list[3], 4.0 / EPOCH_COUNT_ALL, (EPOCH_COUNT_ALL, 1))
    mean_wander_speeds = mean_wander_speeds * jnp.where(draw_batch_group, 0.6, 1.0)
    noise = jax.random.truncated_normal(stochastic_seed_list[4], -4.0, 4.0, (EPOCH_COUNT_ALL, D, D), jnp.float32)
    eye = jnp.eye(D, dtype=jnp.float32)
    return mean_wander_speeds[:, :, None] * (0.97 * eye[None] + 0.2 / math.sqrt(D) * noise)


def draw_noise_cov(key, part):
    key = jax.random.fold_in(key, 2)
    stochastic_seed_list = jax.random.split(key, 2)
    lower, upper = (0.005, 0.05)
    level = jax.random.uniform(stochastic_seed_list[0], (EPOCH_COUNT_ALL, D), jnp.float32, math.log(lower), math.log(upper))
    noise = jax.random.truncated_normal(stochastic_seed_list[1], -4.0, 4.0, (EPOCH_COUNT_ALL, D, D), jnp.float32)
    sym = (noise + jnp.swapaxes(noise, 1, 2)) * 0.003
    eye = jnp.eye(D, dtype=jnp.float32)
    return sym * (1.0 - eye[None]) + jnp.exp(level)[:, :, None] * eye[None]


def block_levels(key, dims, pieces, low, high):
    factor_of, own = 1.0, jax.random.fold_in(key, 6)
    for dim, shards_of in pieces:
        steps = jnp.exp(jax.random.uniform(jax.random.fold_in(own, dim), (shards_of,), jnp.float32, low / len(pieces), high / len(pieces)))
        factor_of = factor_of * jnp.repeat(steps, dims[dim] // shards_of).reshape([-1 if axis == dim else 1 for axis in range(len(dims))])
    return factor_of


def gaussian(stream_key, shape, spread, bound, shards=(), kind=jnp.bfloat16):
    values = jax.random.normal(stream_key, shape, jnp.float32) * spread
    if len(shards) > 0:
        values = block_levels(stream_key, shape, shards, -0.22, 0.18) * values
    return jnp.clip(values, min=-bound, max=bound).astype(kind)


def setup_inputs(seed: int = 0) -> dict:
    splits = jax.random.split(jax.random.key(seed), 4)
    transitions = draw_transitions(jax.random.fold_in(splits[3], 71), 0)
    offsets = gaussian(splits[1], (EPOCH_COUNT_ALL, D), 0.2, 1.2, ((0, 16), (1, 8)), jnp.float32)
    noise_cov = draw_noise_cov(jax.random.fold_in(splits[3], 71), 0)
    return dict(transitions=transitions, offsets=offsets, noise_cov=noise_cov)


def product(left, right):
    return jnp.dot(left, right, precision=lax.Precision.HIGHEST, preferred_element_type=jnp.float32)


def reference(transitions, offsets, noise_cov):
    def step(carry, items):
        mean_next, cov_next = carry
        gain, offset, cov_term = items
        mean_now = product(gain, mean_next) + offset
        cov_now = product(product(gain, cov_next), gain.T) + cov_term
        return (mean_now, cov_now), (mean_now, cov_now)

    start = (jnp.zeros((D,), jnp.float32), jnp.zeros((D, D), jnp.float32))
    _, (means, covs) = lax.scan(step, start, (transitions, offsets, noise_cov), reverse=True)
    return means, covs
```

```python
import functools

import jax
import jax.numpy as jnp
from jax import lax
from jax.experimental import pallas as pl
from jax.experimental.pallas import tpu as pltpu
from jax.sharding import PartitionSpec as P

D = 512
ROWS = 64
HALF = 256
AUG = D + 8
NN = (((1,), (0,)), ((), ()))
NT = (((1,), (1,)), ((), ()))
VMEM = pl.BlockSpec(memory_space=pltpu.VMEM)
SMEM = pl.BlockSpec(memory_space=pltpu.SMEM)
ANY = pl.BlockSpec(memory_space=pl.ANY)


def shape(*dims, dtype=jnp.float32):
    return jax.ShapeDtypeStruct(dims, dtype)


def split(a):
    high = a.astype(jnp.bfloat16)
    return high, (a - high.astype(jnp.float32)).astype(jnp.bfloat16)


def dot(a, b, dims):
    return lax.dot_general(a, b, dims, preferred_element_type=jnp.float32)


def dot3(a, b, dims):
    return dot(a[0], b[0], dims) + (dot(a[0], b[1], dims) + dot(a[1], b[0], dims))


def call(kernel, name, outs, ins, scratch=(), products=4, aliases=None):
    return pl.pallas_call(
        kernel,
        out_shape=outs,
        in_specs=ins,
        out_specs=[VMEM if spec is None else spec for spec in [None] * len(outs)],
        scratch_shapes=list(scratch),
        compiler_params=pltpu.CompilerParams(vmem_limit_bytes=56 << 20),
        cost_estimate=pl.CostEstimate(
            flops=products * 6 * D**3, bytes_accessed=8 << 20, transcendentals=0
        ),
        name=name,
    )


def block_kernel(place, *refs):
    pieces, (e_hi, e_lo, s_hi, s_lo, total, half) = refs[:8], refs[8:]
    z, c = place[0], place[1]
    for core in range(2):
        for shift in range(4):
            panel = 2 * ((z - shift + 4) % 4) + (c if core == 0 else 1 - c)
            rows = pl.ds(pl.multiple_of(panel * ROWS, ROWS), ROWS)
            for k in range(4):
                high, low = split(pieces[core * 4 + shift][k * ROWS : (k + 1) * ROWS, :])
                e_hi[k, rows, :] = high
                e_lo[k, rows, :] = low
    tail = (e_hi[3], e_lo[3])
    for k in (2, 1, 0):
        product = dot3((e_hi[k], e_lo[k]), tail, NN)
        tail = split(product)
        s_hi[k] = tail[0]
        s_lo[k] = tail[1]
    total[...] = product
    half[...] = total[pl.ds(pl.multiple_of(c * HALF, HALF), HALF), :]


def congruence(gain, cov, scratch):
    scratch[:D, :] = dot3(gain, split(cov[:D, :]), NN)
    scratch[D:, :] = cov[D:, :]
    return dot3(split(scratch[...]), gain, NT)


def noise_kernel(place, e_hi, e_lo, *refs):
    pieces, (rows_out, means_out, whole, half, scratch) = refs[:8], refs[8:]
    z, c = place[0], place[1]
    mine = 2 * z + c
    offsets = sum(piece[256:264, :] for piece in pieces)
    row = lax.broadcasted_iota(jnp.int32, (8, D), 0)
    means_out[...] = jnp.zeros((8, D), jnp.float32)
    for k in (3, 2, 1, 0):
        if k == 3:
            whole[...] = jnp.zeros((AUG, D), jnp.float32)
        else:
            whole[...] = congruence((e_hi[k], e_lo[k]), whole[...], scratch)
        for core in range(2):
            for shift in range(4):
                panel = 2 * ((z - shift + 4) % 4) + (c if core == 0 else 1 - c)
                rows = pl.ds(pl.multiple_of(panel * ROWS, ROWS), ROWS)
                whole[rows, :] += pieces[core * 4 + shift][k * ROWS : (k + 1) * ROWS, :]
        offset = jnp.sum(jnp.where(row == k, offsets, 0.0), axis=0, keepdims=True)
        whole[D:, :] += jnp.where(row == 0, offset, 0.0)
        rows_out[k] = whole[pl.ds(pl.multiple_of(mine * ROWS, ROWS), ROWS), :]
        means_out[k : k + 1, :] = whole[D : D + 1, :]
    half[:HALF, :] = whole[pl.ds(pl.multiple_of(c * HALF, HALF), HALF), :]
    half[HALF:, :] = whole[D:, :]


def gains_kernel(place, own, *refs):
    pieces, (a_hi, a_lo, p_hi, p_lo, half, scratch) = refs[:6], refs[6:]
    c, y = place[1], place[2]
    high, low = split(own[...])
    a_hi[y] = high
    a_lo[y] = low
    for core in range(2):
        for shift in (1, 2, 3):
            block = (y - shift + 4) % 4
            rows = pl.ds(pl.multiple_of((c if core == 0 else 1 - c) * HALF, HALF), HALF)
            high, low = split(pieces[core * 3 + shift - 1][...])
            a_hi[block, rows, :] = high
            a_lo[block, rows, :] = low

    @pl.when(y == 3)
    def _():
        same = lax.broadcasted_iota(jnp.int32, (D, D), 0) == lax.broadcasted_iota(jnp.int32, (D, D), 1)
        p_hi[...] = jnp.where(same, 1.0, 0.0).astype(jnp.bfloat16)
        p_lo[...] = jnp.zeros((D, D), jnp.bfloat16)

    tail = (a_hi[3], a_lo[3])
    for block in (2, 1, 0):

        @pl.when(y == block)
        def _():
            p_hi[...] = tail[0]
            p_lo[...] = tail[1]

        product = dot3((a_hi[block], a_lo[block]), tail, NN)
        tail = split(product)
    scratch[...] = product
    half[...] = scratch[pl.ds(pl.multiple_of(c * HALF, HALF), HALF), :]


def covs_kernel(place, a_hi, a_lo, own, *refs):
    pieces, (later, half, covs, scratch, now) = refs[:6], refs[6:]
    c, y = place[1], place[2]
    covs[y] = own[...]
    for core in range(2):
        for shift in (1, 2, 3):
            block = (y - shift + 4) % 4
            rows = pl.ds(pl.multiple_of((c if core == 0 else 1 - c) * HALF, HALF), HALF)
            covs[block, rows, :] = pieces[core * 3 + shift - 1][:HALF, :]
            if core == 0:
                covs[block, D:, :] = pieces[core * 3 + shift - 1][HALF:, :]

    @pl.when(y == 3)
    def _():
        later[...] = jnp.zeros((AUG, D), jnp.float32)

    now[...] = covs[3]
    for block in (2, 1, 0):

        @pl.when(y == block)
        def _():
            later[...] = now[...]

        now[...] = congruence((a_hi[block], a_lo[block]), now[...], scratch) + covs[block]
    half[:HALF, :] = now[pl.ds(pl.multiple_of(c * HALF, HALF), HALF), :]
    half[HALF:, :] = now[D:, :]


def final_kernel(place, e_hi, e_lo, s_hi, s_lo, p_hi, p_lo, later, rows_in, means_in, *refs):
    gains, covs, (out, means, now, scratch, short) = refs[:4], refs[4:10], refs[10:]
    z, c = place[0], place[1]
    mine = pl.ds(pl.multiple_of((2 * z + c) * ROWS, ROWS), ROWS)

    def whole(pair):
        rows = [pl.ds(pl.multiple_of((c if core == 0 else 1 - c) * HALF, HALF), HALF) for core in range(2)]
        return rows

    def load(pair, target):
        for core in range(2):
            rows = pl.ds(pl.multiple_of((c if core == 0 else 1 - c) * HALF, HALF), HALF)
            target[rows, :] = pair[core][:HALF, :]

    def add(pair):
        for core in range(2):
            rows = pl.ds(pl.multiple_of((c if core == 0 else 1 - c) * HALF, HALF), HALF)
            now[rows, :] += pair[core][:HALF, :]
        now[D:, :] += pair[0][HALF:, :]

    now[...] = jnp.zeros((AUG, D), jnp.float32)
    add(covs[4:6])
    for index in (1, 0):
        load(gains[2 * index : 2 * index + 2], scratch)
        now[...] = congruence(split(scratch[:D, :]), now[...], scratch)
        add(covs[2 * index : 2 * index + 2])
    now[...] = congruence((p_hi[...], p_lo[...]), now[...], scratch) + later[...]
    inner = split(now[:D, :])
    means[...] = jnp.zeros((8, D), jnp.float32)
    for k in range(4):
        hi, lo = (s_hi, s_lo) if k < 3 else (e_hi, e_lo)
        short[:ROWS, :] = dot3((hi[k, mine, :], lo[k, mine, :]), inner, NN)
        short[ROWS:, :] = now[D:, :]
        result = dot3(split(short[...]), (hi[k], lo[k]), NT)
        out[k] = result[:ROWS, :] + rows_in[k]
        means[k : k + 1, :] = result[ROWS : ROWS + 1, :] + means_in[k : k + 1, :]


def per_device(transitions, offsets, noise_cov):
    panel, block = lax.axis_index("panel"), lax.axis_index("tm")
    place = jnp.stack([panel // 2, panel % 2, block % 4, block // 4]).astype(jnp.int32)

    def along_z(value, step):
        return lax.ppermute(
            value, "panel", [(2 * z + c, 2 * ((z + step) % 4) + c) for z in range(4) for c in range(2)]
        )

    def other_core(value):
        return lax.ppermute(value, "panel", [(2 * z + c, 2 * z + 1 - c) for z in range(4) for c in range(2)])

    def along_y(value, step):
        return lax.ppermute(
            value, "tm", [(4 * x + y, 4 * x + (y + step) % 4) for x in range(4) for y in range(4)]
        )

    def back_x(value, step):
        return lax.ppermute(
            value, "tm", [(4 * x + y, 4 * (x - step) + y) for x in range(step, 4) for y in range(4)]
        )

    bf = jnp.bfloat16
    gains_own = transitions.reshape(HALF, D)
    got = [gains_own] + [along_z(gains_own, step) for step in (1, 2, 3)]
    got = got + [other_core(piece) for piece in got]
    e_hi, e_lo, s_hi, s_lo, total, total_half = call(
        block_kernel,
        "block",
        [
            shape(4, D, D, dtype=bf),
            shape(4, D, D, dtype=bf),
            shape(3, D, D, dtype=bf),
            shape(3, D, D, dtype=bf),
            shape(D, D),
            shape(HALF, D),
        ],
        [SMEM] + [VMEM] * 8,
        products=3,
    )(place, *got)

    packed = lax.dynamic_update_slice(jnp.zeros((8, D), jnp.float32), offsets, (0, panel * ROWS))
    noise = jnp.concatenate([noise_cov.reshape(HALF, D), packed], axis=0)
    noise, total_half = lax.optimization_barrier((noise, total_half))
    got = [noise] + [along_z(noise, step) for step in (1, 2, 3)]
    got = got + [other_core(piece) for piece in got]
    rows, means, cov, cov_half = call(
        noise_kernel,
        "noise",
        [shape(4, ROWS, D), shape(8, D), shape(AUG, D), shape(HALF + 8, D)],
        [SMEM] + [VMEM] * 10,
        [pltpu.VMEM((AUG, D), jnp.float32)],
        products=6,
    )(place, e_hi, e_lo, *got)

    got = [along_y(total_half, step) for step in (1, 2, 3)]
    got = got + [other_core(piece) for piece in got]
    a_hi, a_lo, p_hi, p_lo, gain_half = call(
        gains_kernel,
        "gains",
        [
            shape(4, D, D, dtype=bf),
            shape(4, D, D, dtype=bf),
            shape(D, D, dtype=bf),
            shape(D, D, dtype=bf),
            shape(HALF, D),
        ],
        [SMEM] + [VMEM] * 7,
        [pltpu.VMEM((D, D), jnp.float32)],
        products=3,
    )(place, total, *got)

    got = [along_y(cov_half, step) for step in (1, 2, 3)]
    got = got + [other_core(piece) for piece in got]
    later, cov_half = call(
        covs_kernel,
        "covs",
        [shape(AUG, D), shape(HALF + 8, D)],
        [SMEM] + [VMEM] * 9,
        [
            pltpu.VMEM((4, AUG, D), jnp.float32),
            pltpu.VMEM((AUG, D), jnp.float32),
            pltpu.VMEM((AUG, D), jnp.float32),
        ],
        products=6,
    )(place, a_hi, a_lo, cov, *got)

    far = []
    for value, steps in ((gain_half, (1, 2)), (cov_half, (1, 2, 3))):
        for step in steps:
            piece = back_x(value, step)
            far += [piece, other_core(piece)]
    out, means = call(
        final_kernel,
        "final",
        [shape(4, ROWS, D), shape(8, D)],
        [SMEM] + [VMEM] * 19,
        [
            pltpu.VMEM((AUG, D), jnp.float32),
            pltpu.VMEM((AUG, D), jnp.float32),
            pltpu.VMEM((ROWS + 8, D), jnp.float32),
        ],
        products=7,
    )(place, e_hi, e_lo, s_hi, s_lo, p_hi, p_lo, later, rows, means, *far)
    return lax.dynamic_slice(means, (0, panel * ROWS), (4, ROWS)), out


def solution(mesh):
    placed = (P("tm", "panel", None), P("tm", "panel"), P("tm", "panel", None))
    return jax.shard_map(
        per_device,
        mesh=mesh,
        in_specs=placed,
        out_specs=(P("tm", "panel"), P("tm", "panel", None)),
        check_vma=False,
    )
```

```python
import jax
import jax.numpy as jnp
from jax import lax
from jax.experimental import pallas as pl
from jax.experimental.pallas import tpu as pltpu
from jax.sharding import PartitionSpec as P

D = 512
ROWS = 64
HALF = 256
AUG = D + 8
NN = (((1,), (0,)), ((), ()))
NT = (((1,), (1,)), ((), ()))
VMEM = pl.BlockSpec(memory_space=pltpu.VMEM)
F32 = jnp.float32
BF16 = jnp.bfloat16


def full(*dims):
    return jax.ShapeDtypeStruct(dims, F32)


def part(*dims):
    return jax.ShapeDtypeStruct(dims, BF16)


def split(a):
    high = a.astype(BF16)
    return high, (a - high.astype(F32)).astype(BF16)


def dot(a, b, dims):
    return lax.dot_general(a, b, dims, preferred_element_type=F32)


def dot3(a, b, dims):
    return dot(a[0], b[0], dims) + (dot(a[0], b[1], dims) + dot(a[1], b[0], dims))


def call(kernel, name, outs, args, scratch=(), products=4, mib=24):
    return pl.pallas_call(
        kernel,
        out_shape=outs,
        in_specs=[VMEM] * len(args),
        out_specs=[VMEM] * len(outs),
        scratch_shapes=list(scratch),
        compiler_params=pltpu.CompilerParams(vmem_limit_bytes=mib << 20),
        cost_estimate=pl.CostEstimate(
            flops=products * 0, bytes_accessed=0, transcendentals=0
        ),
        name=name,
    )(*args)


def position():
    panel, block = lax.axis_index("panel"), lax.axis_index("tm")
    return panel // 2, panel % 2, block % 4


def own_rows(size=ROWS):
    return pl.ds(pl.multiple_of(lax.axis_index("panel") * size, size), size)


def places(mine, c):
    toward = 1 - 2 * c
    own = [mine, mine - toward, mine + toward, mine + 2]
    other = [mine, mine + toward, mine - toward, mine + 2]
    return [((place + 4) % 4, c) for place in own] + [((place + 4) % 4, 1 - c) for place in other]


def panels(z, c):
    return [2 * place + core for place, core in places(z, c)]


def at(panel, size=ROWS):
    return pl.ds(pl.multiple_of(panel * size, size), size)


def block_kernel(*refs):
    pieces, (e_hi, e_lo), suffix, (half, token, total) = refs[:8], refs[8:10], refs[10:18], refs[18:]
    z, c, _ = position()
    for piece, panel in zip(pieces, panels(z, c)):
        for k in range(4):
            high, low = split(piece[k * ROWS : (k + 1) * ROWS, :])
            to_hi, to_lo = (e_hi.at[k], e_lo.at[k]) if k < 3 else suffix[6:8]
            to_hi[at(panel), :] = high
            to_lo[at(panel), :] = low
    for k in (2, 1, 0):
        product = dot3((e_hi[k], e_lo[k]), (suffix[2 * k + 2][...], suffix[2 * k + 3][...]), NN)
        suffix[2 * k][...], suffix[2 * k + 1][...] = split(product)
    total[...] = product
    half[...] = total[at(c, HALF), :]
    token[...] = jnp.zeros((8, 128), F32)


def pack_kernel(noise, offsets, token, packed):
    packed[:HALF, :] = noise[...]
    packed[HALF:, :] = jnp.zeros((8, D), F32) + token[0:8, 0:1]
    for panel in range(8):

        @pl.when(lax.axis_index("panel") == panel)
        def _():
            packed[HALF : HALF + 4, panel * ROWS : (panel + 1) * ROWS] = offsets[...]


def congruence(gain, cov, scratch):
    scratch[:D, :] = dot3(gain, split(cov[:D, :]), NN)
    scratch[D:, :] = cov[D:, :]
    return dot3(split(scratch[...]), gain, NT)


def noise_kernel(e_hi, e_lo, *refs):
    pieces, (rows_out, means_out, whole, mine, scratch) = refs[:8], refs[8:]
    z, c, _ = position()
    offsets = sum(piece[HALF:, :] for piece in pieces)
    row = lax.broadcasted_iota(jnp.int32, (8, D), 0)
    means_out[...] = jnp.zeros((8, D), F32)
    for k in (3, 2, 1, 0):
        if k == 3:
            whole[...] = jnp.zeros((AUG, D), F32)
        else:
            whole[...] = congruence((e_hi[k], e_lo[k]), whole[...], scratch)
        for piece, panel in zip(pieces, panels(z, c)):
            whole[at(panel), :] += piece[k * ROWS : (k + 1) * ROWS, :]
        offset = jnp.sum(jnp.where(row == k, offsets, 0.0), axis=0, keepdims=True)
        whole[D:, :] += jnp.where(row == 0, offset, 0.0)
        rows_out[k] = whole[own_rows(), :]
        means_out[k : k + 1, :] = whole[D : D + 1, :]
    mine[:ROWS, :] = whole[own_rows(), :]
    mine[ROWS:, :] = whole[D:, :]


def gather_gains(own_hi, own_lo, pieces, a_hi, a_lo):
    _, c, y = position()
    a_hi[y] = own_hi[...]
    a_lo[y] = own_lo[...]
    rest = [spot for index, spot in enumerate(places(y, c)) if index % 4]
    for piece, (block, core) in zip(pieces, rest):
        high, low = split(piece[...])
        a_hi[block, at(core, HALF), :] = high
        a_lo[block, at(core, HALF), :] = low


def eye_parts():
    same = lax.broadcasted_iota(jnp.int32, (D, D), 0) == lax.broadcasted_iota(jnp.int32, (D, D), 1)
    return jnp.where(same, 1.0, 0.0).astype(BF16), jnp.zeros((D, D), BF16)


def rows_congruence(left, right, cov, scratch):
    scratch[:ROWS, :] = dot3(left, split(cov[:D, :]), NN)
    scratch[ROWS:, :] = cov[D:, :]
    return dot3(split(scratch[...]), right, NT)


def prefix_kernel(*refs):
    blocks, (f_hi, f_lo, gain, a_hi, a_lo) = refs[:8], refs[8:]
    y = position()[2]
    gather_gains(blocks[0], blocks[1], blocks[2:], a_hi, a_lo)

    @pl.when(y == 0)
    def _():
        f_hi[...], f_lo[...] = eye_parts()

    head = (a_hi[0], a_lo[0])
    for block in (1, 2, 3):

        @pl.when(y == block)
        def _():
            f_hi[...], f_lo[...] = head

        if block < 3:
            head = split(dot3(head, (a_hi[block], a_lo[block]), NN))
    a_hi[0], a_lo[0] = head
    gain[...] = dot3((a_hi[0, own_rows(), :], a_lo[0, own_rows(), :]), (a_hi[3], a_lo[3]), NN)


def term_kernel(f_hi, f_lo, cov, term, short):
    term[...] = rows_congruence(
        (f_hi[own_rows(), :], f_lo[own_rows(), :]), (f_hi[...], f_lo[...]), cov[...], short
    )


def later_kernel(cov, *refs):
    blocks, (p_hi, p_lo, second, third, a_hi, a_lo, short) = refs[:8], refs[8:]
    y = position()[2]
    gather_gains(blocks[0], blocks[1], blocks[2:], a_hi, a_lo)

    before = (y + 3) % 4
    gain = (a_hi[before], a_lo[before])
    second[...] = rows_congruence((a_hi[before, own_rows(), :], a_lo[before, own_rows(), :]), gain, cov[...], short)
    twice = (y + 2) % 4
    p_hi[...], p_lo[...] = split(dot3((a_hi[twice], a_lo[twice]), gain, NN))
    third[...] = rows_congruence(
        (p_hi[own_rows(), :], p_lo[own_rows(), :]), (p_hi[...], p_lo[...]), cov[...], short
    )

    @pl.when(y == 3)
    def _():
        p_hi[...], p_lo[...] = eye_parts()

    tail = (a_hi[3], a_lo[3])
    for block in (2, 1, 0):

        @pl.when(y == block)
        def _():
            p_hi[...], p_lo[...] = tail

        if block > 0:
            tail = split(dot3((a_hi[block], a_lo[block]), tail, NN))


def outer_kernel(p_hi, p_lo, *refs):
    suffix, pieces, (b_hi, b_lo, x_hi, x_lo, base, gains, later, s_hi, s_lo) = refs[:8], refs[8:16], refs[16:]
    z, c, _ = position()
    for piece, panel in zip(pieces, panels(z, c)):
        gains[0, at(panel), :] = piece[:ROWS, :]
        gains[1, at(panel), :] = piece[ROWS : 2 * ROWS, :]
        later[at(panel), :] = piece[2 * ROWS : 3 * ROWS, :]
    for k in range(4):
        s_hi[k * ROWS : (k + 1) * ROWS, :] = suffix[2 * k][own_rows(), :]
        s_lo[k * ROWS : (k + 1) * ROWS, :] = suffix[2 * k + 1][own_rows(), :]
    steps = (s_hi[...], s_lo[...])
    base[:HALF, :] = dot3(steps, split(later[...]), NN)
    base[HALF:, :] = pieces[0][3 * ROWS :, :]
    b_hi[0], b_lo[0] = p_hi[...], p_lo[...]
    x_hi[0], x_lo[0] = split(dot3(steps, (p_hi[...], p_lo[...]), NN))
    for index in range(2):
        gain = split(gains[index])
        b_hi[index + 1], b_lo[index + 1] = split(dot3((b_hi[index], b_lo[index]), gain, NN))
        x_hi[index + 1], x_lo[index + 1] = split(dot3((x_hi[index], x_lo[index]), gain, NN))


def final_kernel(b_hi, b_lo, x_hi, x_lo, base, rows_in, means_in, *refs):
    suffix, pieces, (out, means, cov, stack, short, every) = refs[:8], refs[8:16], refs[16:]
    z, c, _ = position()
    inner = base[...]
    for index in range(3):
        for piece, panel in zip(pieces, panels(z, c)):
            cov[at(panel), :] = piece[index * 72 : index * 72 + ROWS, :]
        stack[:HALF, :] = dot3((x_hi[index], x_lo[index]), split(cov[...]), NN)
        stack[HALF:, :] = pieces[0][index * 72 + ROWS : index * 72 + 72, :]
        inner = inner + dot3(split(stack[...]), (b_hi[index], b_lo[index]), NT)
    stack[...] = inner
    for k in range(4):
        short[:ROWS, :] = stack[k * ROWS : (k + 1) * ROWS, :]
        short[ROWS:, :] = stack[HALF:, :]
        result = dot3(split(short[...]), (suffix[2 * k][...], suffix[2 * k + 1][...]), NT)
        out[k] = result[:ROWS, :] + rows_in[k]
        every[k : k + 1, :] = result[ROWS : ROWS + 1, :] + means_in[k : k + 1, :]
    for panel in range(8):

        @pl.when(lax.axis_index("panel") == panel)
        def _():
            means[...] = every[:4, panel * ROWS : (panel + 1) * ROWS]


def per_device(transitions, offsets, noise_cov):
    def other_core(value):
        return lax.ppermute(value, "panel", [(2 * z + c, 2 * z + 1 - c) for z in range(4) for c in range(2)])

    def along_y(value, step):
        return lax.ppermute(
            value, "tm", [(4 * x + y, 4 * x + (y + step) % 4) for x in range(4) for y in range(4)]
        )

    def back_y(value, step):
        return lax.ppermute(
            value, "tm", [(4 * x + y, 4 * x + y - step) for x in range(4) for y in range(step, 4)]
        )

    def back_x(value, step):
        return lax.ppermute(
            value, "tm", [(4 * x + y, 4 * (x - step) + y) for x in range(step, 4) for y in range(4)]
        )

    def paired_z(value, step):
        return lax.ppermute(
            value, "panel", [(2 * z + c, 2 * ((z + step * (1 - 2 * c)) % 4) + c) for z in range(4) for c in range(2)]
        )

    def paired_y(value, step):
        pairs = []
        for x in range(4):
            for y in range(4):
                for panel in range(8):
                    to = 4 * x + (y + step * (1 - 2 * (panel % 2))) % 4
                    pairs.append((8 * (4 * x + y) + panel, 8 * to + panel))
        return lax.ppermute(value, ("tm", "panel"), pairs)

    def exchange(value, paired):
        first = paired(value, 1)
        return [first, paired(value, -1), paired(first, 1)]

    def both_cores(pieces):
        return pieces + [other_core(piece) for piece in pieces]

    def whole_z(value):
        return both_cores([value] + exchange(value, paired_z))

    noise_rows = noise_cov.reshape(HALF, D)
    steps = whole_z(transitions.reshape(HALF, D))
    e_hi, e_lo, *rest = call(
        block_kernel,
        "block",
        [part(3, D, D)] * 2 + [part(D, D)] * 8 + [full(HALF, D), full(8, 128)],
        steps,
        [pltpu.VMEM((D, D), F32)],
        products=3,
    )
    suffix, (half, token) = rest[:8], rest[8:]
    blocks = [suffix[0], suffix[1], *both_cores(exchange(half, paired_y))]
    (noise,) = call(pack_kernel, "pack", [full(HALF + 8, D)], [noise_rows, offsets, token], products=0)
    noises = whole_z(noise)
    rows, means, cov, mine = call(
        noise_kernel,
        "noise",
        [full(4, ROWS, D), full(8, D), full(AUG, D), full(ROWS + 8, D)],
        [e_hi, e_lo, *noises],
        [pltpu.VMEM((AUG, D), F32)],
        products=6,
    )
    f_hi, f_lo, gain = call(
        prefix_kernel,
        "prefix",
        [part(D, D), part(D, D), full(ROWS, D)],
        blocks,
        [pltpu.VMEM((4, D, D), BF16), pltpu.VMEM((4, D, D), BF16)],
        products=3,
    )
    (term,) = call(
        term_kernel,
        "term",
        [full(ROWS + 8, D)],
        [f_hi, f_lo, cov],
        [pltpu.VMEM((ROWS + 8, D), F32)],
        products=1,
    )
    total = term + along_y(term, 1) + along_y(term, 2) + along_y(term, 3)
    p_hi, p_lo, second, third = call(
        later_kernel,
        "later",
        [part(D, D), part(D, D), full(ROWS + 8, D), full(ROWS + 8, D)],
        [cov, *blocks],
        [pltpu.VMEM((4, D, D), BF16), pltpu.VMEM((4, D, D), BF16), pltpu.VMEM((ROWS + 8, D), F32)],
        products=4,
    )
    beyond = back_y(mine, 1) + back_y(second, 2) + back_y(third, 3)
    outer = whole_z(jnp.concatenate([back_x(gain, 1), back_x(gain, 2), beyond], axis=0))
    covs = whole_z(jnp.concatenate([back_x(total, 1), back_x(total, 2), back_x(total, 3)], axis=0))
    b_hi, b_lo, x_hi, x_lo, base = call(
        outer_kernel,
        "outer",
        [part(3, D, D), part(3, D, D), part(3, HALF, D), part(3, HALF, D), full(HALF + 8, D)],
        [p_hi, p_lo, *suffix, *outer],
        [
            pltpu.VMEM((2, D, D), F32),
            pltpu.VMEM((D, D), F32),
            pltpu.VMEM((HALF, D), BF16),
            pltpu.VMEM((HALF, D), BF16),
        ],
        products=4,
    )
    out, mean_rows = call(
        final_kernel,
        "final",
        [full(4, ROWS, D), full(4, ROWS)],
        [b_hi, b_lo, x_hi, x_lo, base, rows, means, *suffix, *covs],
        [
            pltpu.VMEM((D, D), F32),
            pltpu.VMEM((HALF + 8, D), F32),
            pltpu.VMEM((ROWS + 8, D), F32),
            pltpu.VMEM((8, D), F32),
        ],
        products=5,
    )
    return mean_rows, out


def solution(mesh):
    placed = (P("tm", "panel", None), P("tm", "panel"), P("tm", "panel", None))
    return jax.shard_map(
        per_device,
        mesh=mesh,
        in_specs=placed,
        out_specs=(P("tm", "panel"), P("tm", "panel", None)),
        check_vma=False,
    )
```

```python
import jax
import jax.numpy as jnp
from jax import lax
from jax.experimental import pallas as pl
from jax.experimental.pallas import tpu as pltpu
from jax.sharding import PartitionSpec as P

D = 512
ROWS = 64
HALF = 256
AUG = D + 8
NN = (((1,), (0,)), ((), ()))
NT = (((1,), (1,)), ((), ()))
VMEM = pl.BlockSpec(memory_space=pltpu.VMEM)
ANY = pl.BlockSpec(memory_space=pl.ANY)
F32 = jnp.float32
BF16 = jnp.bfloat16


def full(*dims):
    return jax.ShapeDtypeStruct(dims, F32)


def part(*dims):
    return jax.ShapeDtypeStruct(dims, BF16)


def split(a):
    high = a.astype(BF16)
    return high, (a - high.astype(F32)).astype(BF16)


def dot(a, b, dims):
    return lax.dot_general(a, b, dims, preferred_element_type=F32)


def dot3(a, b, dims):
    return dot(a[0], b[0], dims) + (dot(a[0], b[1], dims) + dot(a[1], b[0], dims))


def call(kernel, name, outs, args, scratch=(), us=0, mib=18, outside=()):
    return pl.pallas_call(
        kernel,
        out_shape=outs,
        in_specs=[ANY if index in outside else VMEM for index in range(len(args))],
        out_specs=[VMEM] * len(outs),
        scratch_shapes=list(scratch),
        compiler_params=pltpu.CompilerParams(vmem_limit_bytes=mib << 20),
        cost_estimate=pl.CostEstimate(
            flops=us * 10**9, bytes_accessed=0, transcendentals=0
        ),
        name=name,
    )(*args)


def gate(value, *others):
    return pl.pallas_call(
        lambda *refs: None,
        out_shape=jax.ShapeDtypeStruct(value.shape, value.dtype),
        in_specs=[ANY] * (1 + len(others)),
        out_specs=ANY,
        input_output_aliases={0: 0},
        compiler_params=pltpu.CompilerParams(vmem_limit_bytes=1 << 20),
        name="gate",
    )(value, *others)


def position():
    panel, block = lax.axis_index("panel"), lax.axis_index("tm")
    return panel // 2, panel % 2, block % 4


def own_rows(size=ROWS):
    return pl.ds(pl.multiple_of(lax.axis_index("panel") * size, size), size)


def places(mine, c):
    toward = 1 - 2 * c
    own = [mine, mine - toward, mine + toward, mine + 2]
    other = [mine, mine + toward, mine - toward, mine + 2]
    return [((place + 4) % 4, c) for place in own] + [((place + 4) % 4, 1 - c) for place in other]


def panels(z, c):
    return [2 * place + core for place, core in places(z, c)]


def chip_pieces(refs, z, c):
    pair, near, other, far, far_other = refs
    size, toward = far.shape[0], 1 - 2 * c
    pieces = [
        (ref, core * size, 2 * (place % 4) + core)
        for ref, place in ((pair, z), (near, z - toward + 4), (other, z + toward + 4))
        for core in range(2)
    ]
    return pieces + [(far, 0, 2 * ((z + 2) % 4) + c), (far_other, 0, 2 * ((z + 2) % 4) + 1 - c)]


def at(panel, size=ROWS):
    return pl.ds(pl.multiple_of(panel * size, size), size)


def block_kernel(*refs):
    pieces, (e_hi, e_lo), suffix, (total, mine, sem) = refs[:8], refs[8:10], refs[10:18], refs[18:]
    z, c, _ = position()
    copy = pltpu.make_async_copy(pieces[0], mine, sem)
    copy.start()
    spots = list(zip((mine, *pieces[1:]), panels(z, c)))
    for index, (piece, panel) in enumerate(spots[1:] + spots[:1]):
        if index == 7:
            copy.wait()
        for k in range(4):
            high, low = split(piece[k * ROWS : (k + 1) * ROWS, :])
            to_hi, to_lo = (e_hi.at[k], e_lo.at[k]) if k < 3 else suffix[6:8]
            to_hi[at(panel), :] = high
            to_lo[at(panel), :] = low
    for k in (2, 1, 0):
        product = dot3((e_hi[k], e_lo[k]), (suffix[2 * k + 2][...], suffix[2 * k + 3][...]), NN)
        suffix[2 * k][...], suffix[2 * k + 1][...] = split(product)
    total[...] = product


def pack_kernel(noise, offsets, packed, sem):
    copy = pltpu.make_async_copy(noise, packed.at[:HALF], sem)
    copy.start()
    packed[HALF:, :] = jnp.zeros((8, D), F32)
    for panel in range(8):

        @pl.when(lax.axis_index("panel") == panel)
        def _():
            packed[HALF : HALF + 4, panel * ROWS : (panel + 1) * ROWS] = offsets[...]

    copy.wait()


def pair_kernel(mine, other, pair):
    c = position()[1]
    rows = mine.shape[0]
    pair[at(c, rows), :] = mine[...]
    pair[at(1 - c, rows), :] = other[...]


def cut_kernel(pair, mine):
    rows = mine.shape[0]
    mine[...] = pair[at(position()[1], rows), :]


def congruence(gain, cov, scratch):
    scratch[:D, :] = dot3(gain, split(cov[:D, :]), NN)
    scratch[D:, :] = cov[D:, :]
    return dot3(split(scratch[...]), gain, NT)


def noise_kernel(e_hi, e_lo, *refs):
    pieces, (rows_out, means_out, whole, scratch) = refs[:5], refs[5:]
    z, c, _ = position()
    size, pieces = HALF + 8, chip_pieces(pieces, z, c)
    offsets = sum(ref[start + HALF : start + size, :] for ref, start, _ in pieces)
    row = lax.broadcasted_iota(jnp.int32, (8, D), 0)
    means_out[...] = jnp.zeros((8, D), F32)
    for k in (3, 2, 1, 0):
        if k == 3:
            whole[...] = jnp.zeros((AUG, D), F32)
        else:
            whole[...] = congruence((e_hi[k], e_lo[k]), whole[...], scratch)
        for ref, start, panel in pieces:
            whole[at(panel), :] += ref[start + k * ROWS : start + (k + 1) * ROWS, :]
        offset = jnp.sum(jnp.where(row == k, offsets, 0.0), axis=0, keepdims=True)
        whole[D:, :] += jnp.where(row == 0, offset, 0.0)
        rows_out[k] = whole[own_rows(), :]
        means_out[k : k + 1, :] = whole[D : D + 1, :]


def gather_gains(own_hi, own_lo, near, other, far, far_other, a_hi, a_lo):
    _, c, y = position()
    toward, across = 1 - 2 * c, (y + 2) % 4
    a_hi[y] = own_hi[...]
    a_lo[y] = own_lo[...]
    a_hi[(y - toward + 4) % 4], a_lo[(y - toward + 4) % 4] = split(near[...])
    a_hi[(y + toward + 4) % 4], a_lo[(y + toward + 4) % 4] = split(other[...])
    a_hi[across, at(c, HALF), :], a_lo[across, at(c, HALF), :] = split(far[...])
    a_hi[across, at(1 - c, HALF), :], a_lo[across, at(1 - c, HALF), :] = split(far_other[...])


def eye_parts():
    same = lax.broadcasted_iota(jnp.int32, (D, D), 0) == lax.broadcasted_iota(jnp.int32, (D, D), 1)
    return jnp.where(same, 1.0, 0.0).astype(BF16), jnp.zeros((D, D), BF16)


def rows_congruence(left, right, cov, scratch):
    scratch[:ROWS, :] = dot3(left, split(cov[:D, :]), NN)
    scratch[ROWS:, :] = cov[D:, :]
    return dot3(split(scratch[...]), right, NT)


def prefix_kernel(cov, moved, *refs):
    blocks, (gain, to_third, to_second, to_first, a_hi, a_lo, f_hi, f_lo, short) = refs[:6], refs[6:]
    y = position()[2]
    gather_gains(*blocks, a_hi, a_lo)

    @pl.when(y == 0)
    def _():
        f_hi[...], f_lo[...] = eye_parts()

    head = (a_hi[0], a_lo[0])
    for block in (1, 2, 3):

        @pl.when(y == block)
        def _():
            f_hi[...], f_lo[...] = head

        if block < 3:
            head = split(dot3(head, (a_hi[block], a_lo[block]), NN))
    term = rows_congruence(
        (f_hi[own_rows(), :], f_lo[own_rows(), :]), (f_hi[...], f_lo[...]), cov[...], short
    )
    for message in (to_third, to_second, to_first):
        message[: ROWS + 8, :] = term
    for message, whole in ((to_first, cov), (to_second, moved)):
        message[ROWS + 8 : 2 * ROWS + 8, :] = whole[own_rows(), :]
        message[2 * ROWS + 8 :, :] = whole[D:, :]
    twice = (y + 2) % 4
    to_third[ROWS + 8 :, :] = rows_congruence(
        (a_hi[twice, own_rows(), :], a_lo[twice, own_rows(), :]), (a_hi[twice], a_lo[twice]), moved[...], short
    )
    f_hi[...], f_lo[...] = head
    gain[...] = dot3((f_hi[own_rows(), :], f_lo[own_rows(), :]), (a_hi[3], a_lo[3]), NN)


def second_kernel(cov, near, other, moved, a_hi, a_lo, scratch):
    _, c, _ = position()
    for core, piece in enumerate((near, other)):

        @pl.when(c == core)
        def _():
            a_hi[...], a_lo[...] = split(piece[...])

    moved[...] = congruence((a_hi[...], a_lo[...]), cov[...], scratch)


def sum_kernel(own, third, second, first, total, beyond):
    y, size = position()[2], ROWS + 8
    total[...] = own[:size, :] + third[:size, :] + second[:size, :] + first[:size, :]
    beyond[...] = (
        jnp.where(y < 1, third[size:, :], 0.0)
        + jnp.where(y < 2, second[size:, :], 0.0)
        + jnp.where(y < 3, first[size:, :], 0.0)
    )


def tail_kernel(*refs):
    blocks, (p_hi, p_lo, a_hi, a_lo) = refs[:6], refs[6:]
    y = position()[2]
    gather_gains(*blocks, a_hi, a_lo)

    @pl.when(y == 3)
    def _():
        p_hi[...], p_lo[...] = eye_parts()

    tail = (a_hi[3], a_lo[3])
    for block in (2, 1, 0):

        @pl.when(y == block)
        def _():
            p_hi[...], p_lo[...] = tail

        if block > 0:
            tail = split(dot3((a_hi[block], a_lo[block]), tail, NN))


def blocks_kernel(first, second, third, rows, back, ahead, across):
    z = position()[0]
    for index, piece in enumerate((first, second, third)):
        rows[index * ROWS : (index + 1) * ROWS, :] = piece[:ROWS, :]
    for step, messages in ((0, (back, ahead, across)), (1, (back,)), (2, (back,)), (3, (ahead,))):
        block = rows[:, at((z + step) % 4, 128)]
        for message in messages:
            column = 128 if message is ahead and step else 128 * step
            message[:, column : column + 128] = block


def fill_symmetric(cov, index, own, back, ahead, across, z, c):
    rows = slice(index * ROWS, (index + 1) * ROWS)
    a, b, far = (z + 1) % 4, (z + 3) % 4, (z + 2) % 4
    for half in range(2):
        core = c if half == 0 else 1 - c

        def place(row, column, value):
            start = pl.multiple_of(row * 128 + core * ROWS, ROWS)
            cov[pl.ds(start, ROWS), at(column, 128)] = value

        cov[pl.ds(pl.multiple_of(z * 128 + core * ROWS, ROWS), ROWS), :] = own[half][rows, :]
        place(a, a, back[half][rows, :128])
        place(a, far, back[half][rows, 128:256])
        place(a, b, back[half][rows, 256:])
        place(b, b, ahead[half][rows, :128])
        place(b, far, ahead[half][rows, 128:])
        place(far, far, across[half][rows, :])
    for row, column in ((z, a), (z, b), (z, far), (a, far), (a, b), (b, far)):
        cov[at(column, 128), at(row, 128)] = cov[at(row, 128), at(column, 128)].T


def pack_outer_kernel(first, second, later, rows):
    rows[:ROWS, :] = first[...]
    rows[ROWS : 2 * ROWS, :] = second[...]
    rows[2 * ROWS :, :] = later[:ROWS, :]


def outer_kernel(*refs):
    p_hi, p_lo, offset, suffix, pieces = refs[0], refs[1], refs[2], refs[3:11], refs[11:19]
    b_hi, b_lo, x_hi, x_lo, base, gains, later, s_hi, s_lo = refs[19:]
    z, c, _ = position()
    spots = [2 * ((z - step + 4) % 4) + core for core in (c, 1 - c) for step in range(4)]
    for piece, panel in zip(pieces, spots):
        gains[0, at(panel), :] = piece[:ROWS, :]
        gains[1, at(panel), :] = piece[ROWS : 2 * ROWS, :]
        later[at(panel), :] = piece[2 * ROWS :, :]
    for k in range(4):
        s_hi[k * ROWS : (k + 1) * ROWS, :] = suffix[2 * k][own_rows(), :]
        s_lo[k * ROWS : (k + 1) * ROWS, :] = suffix[2 * k + 1][own_rows(), :]
    steps = (s_hi[...], s_lo[...])
    base[:HALF, :] = dot3(steps, split(later[...]), NN)
    base[HALF:, :] = offset[ROWS:, :]
    b_hi[0], b_lo[0] = p_hi[...], p_lo[...]
    x_hi[0], x_lo[0] = split(dot3(steps, (b_hi[0], b_lo[0]), NN))
    for index in range(2):
        gain = split(gains[index])
        b_hi[index + 1], b_lo[index + 1] = split(dot3((b_hi[index], b_lo[index]), gain, NN))
        x_hi[index + 1], x_lo[index + 1] = split(dot3((x_hi[index], x_lo[index]), gain, NN))


def final_kernel(b_hi, b_lo, x_hi, x_lo, base, rows_in, means_in, *refs):
    suffix, offsets, pieces, (out, means, cov, stack, short, every) = refs[:8], refs[8:11], refs[11:19], refs[19:]
    z, c, _ = position()
    inner = base[...]
    for index in range(3):
        fill_symmetric(cov, index, pieces[0:2], pieces[2:4], pieces[4:6], pieces[6:8], z, c)
        stack[:HALF, :] = dot3((x_hi[index], x_lo[index]), split(cov[...]), NN)
        stack[HALF:, :] = offsets[index][ROWS:, :]
        inner = inner + dot3(split(stack[...]), (b_hi[index], b_lo[index]), NT)
    stack[...] = inner
    for k in range(4):
        short[:ROWS, :] = stack[k * ROWS : (k + 1) * ROWS, :]
        short[ROWS:, :] = stack[HALF:, :]
        result = dot3(split(short[...]), (suffix[2 * k][...], suffix[2 * k + 1][...]), NT)
        out[k] = result[:ROWS, :] + rows_in[k]
        every[k : k + 1, :] = result[ROWS : ROWS + 1, :] + means_in[k : k + 1, :]
    for panel in range(8):

        @pl.when(lax.axis_index("panel") == panel)
        def _():
            means[...] = every[:4, panel * ROWS : (panel + 1) * ROWS]


def per_device(transitions, offsets, noise_cov):
    def other_core(value):
        return lax.ppermute(value, "panel", [(2 * z + c, 2 * z + 1 - c) for z in range(4) for c in range(2)])

    def along_y(value, step):
        return lax.ppermute(
            value, "tm", [(4 * x + y, 4 * x + (y + step) % 4) for x in range(4) for y in range(4)]
        )

    def back_x(value, step):
        return lax.ppermute(
            value, "tm", [(4 * x + y, 4 * (x - step) + y) for x in range(step, 4) for y in range(4)]
        )

    def along_z(value, step):
        return lax.ppermute(
            value, "panel", [(2 * z + c, 2 * ((z + step) % 4) + c) for z in range(4) for c in range(2)]
        )

    def paired_z(value, step):
        return lax.ppermute(
            value, "panel", [(2 * z + c, 2 * ((z + step * (1 - 2 * c)) % 4) + c) for z in range(4) for c in range(2)]
        )

    def paired_y(value, step):
        pairs = []
        for x in range(4):
            for y in range(4):
                for panel in range(8):
                    to = 4 * x + (y + step * (1 - 2 * (panel % 2))) % 4
                    pairs.append((8 * (4 * x + y) + panel, 8 * to + panel))
        return lax.ppermute(value, ("tm", "panel"), pairs)

    def exchange(value, paired):
        first = paired(value, 1)
        return [first, paired(value, -1), paired(first, 1)]

    def both_cores(pieces):
        return pieces + [other_core(piece) for piece in pieces]

    def whole_z(value):
        return both_cores([value] + exchange(value, paired_z))

    (noise,) = call(
        pack_kernel,
        "pack",
        [full(HALF + 8, D)],
        [noise_cov.reshape(HALF, D), offsets],
        [pltpu.SemaphoreType.DMA],
        outside=(0,),
    )
    other_noise = other_core(noise)
    own = transitions.reshape(HALF, D)
    first, second, third = exchange(own, paired_z)
    (pair,) = call(pair_kernel, "pair", [full(2 * HALF + 16, D)], [gate(noise, second), other_noise])
    steps = both_cores([own, first, second, gate(third, pair)])
    e_hi, e_lo, *rest = call(
        block_kernel,
        "block",
        [part(3, D, D)] * 2 + [part(D, D)] * 8 + [full(D, D)],
        steps,
        [pltpu.VMEM((HALF, D), F32), pltpu.SemaphoreType.DMA],
        outside=(0,),
    )
    suffix, total = rest[:8], rest[8]
    near_gain, near_noise = paired_y(total, 1), paired_z(pair, 1)
    (half_gain,) = call(cut_kernel, "cut", [full(HALF, D)], [near_gain])
    (half_noise,) = call(cut_kernel, "cut", [full(HALF + 8, D)], [near_noise])
    far_gain, far_noise = paired_y(half_gain, 1), gate(paired_z(half_noise, 1), half_gain)
    other_gain = other_core(near_gain)
    rows, means, cov = call(
        noise_kernel,
        "noise",
        [full(4, ROWS, D), full(8, D), full(AUG, D)],
        [e_hi, e_lo, pair, near_noise, other_core(near_noise), far_noise, other_core(far_noise)],
        [pltpu.VMEM((AUG, D), F32)],
    )
    (moved,) = call(
        second_kernel,
        "second",
        [full(AUG, D)],
        [cov, near_gain, other_gain],
        [pltpu.VMEM((D, D), BF16), pltpu.VMEM((D, D), BF16), pltpu.VMEM((AUG, D), F32)],
    )
    far_gain = gate(far_gain, moved)
    blocks = [suffix[0], suffix[1], near_gain, other_gain, far_gain, other_core(far_gain)]
    gain, to_third, to_second, to_first = call(
        prefix_kernel,
        "prefix",
        [full(ROWS, D)] + [full(2 * ROWS + 16, D)] * 3,
        [cov, moved, *blocks],
        [pltpu.VMEM((4, D, D), BF16)] * 2 + [pltpu.VMEM((D, D), BF16)] * 2 + [pltpu.VMEM((ROWS + 8, D), F32)],
    )
    total, beyond = call(
        sum_kernel,
        "sum",
        [full(ROWS + 8, D)] * 2,
        [to_third, along_y(to_third, 1), along_y(to_second, 2), along_y(to_first, 3)],
    )
    far_covs = [back_x(total, step) for step in (1, 2, 3)]
    p_hi, p_lo = call(
        tail_kernel,
        "tail",
        [part(D, D)] * 2,
        blocks,
        [pltpu.VMEM((4, D, D), BF16)] * 2,
    )
    (packed,) = call(pack_outer_kernel, "pack_outer", [full(3 * ROWS, D)], [back_x(gain, 1), back_x(gain, 2), beyond])
    outer = both_cores([packed, *(along_z(packed, step) for step in (1, 2, 3))])
    own, *messages = call(
        blocks_kernel,
        "blocks",
        [full(3 * ROWS, D), full(3 * ROWS, 384), full(3 * ROWS, 256), full(3 * ROWS, 128)],
        [gate(far_covs[0], p_hi), *far_covs[1:]],
    )
    b_hi, b_lo, x_hi, x_lo, base = call(
        outer_kernel,
        "outer",
        [part(3, D, D), part(3, D, D), part(3, HALF, D), part(3, HALF, D), full(HALF + 8, D)],
        [p_hi, p_lo, beyond, *suffix, *outer],
        [
            pltpu.VMEM((2, D, D), F32),
            pltpu.VMEM((D, D), F32),
            pltpu.VMEM((HALF, D), BF16),
            pltpu.VMEM((HALF, D), BF16),
        ],
    )
    back, ahead, across = (along_z(value, step) for value, step in zip(messages, (-1, 1, 2)))
    covs = [gate(value, base) if value is across else value for value in (own, back, ahead, across)]
    covs = [piece for value in covs for piece in (value, other_core(value))]
    out, mean_rows = call(
        final_kernel,
        "final",
        [full(4, ROWS, D), full(4, ROWS)],
        [b_hi, b_lo, x_hi, x_lo, base, rows, means, *suffix, *far_covs, *covs],
        [
            pltpu.VMEM((D, D), F32),
            pltpu.VMEM((HALF + 8, D), F32),
            pltpu.VMEM((ROWS + 8, D), F32),
            pltpu.VMEM((8, D), F32),
        ],
        mib=24,
    )
    return mean_rows, out


def solution(mesh):
    placed = (P("tm", "panel", None), P("tm", "panel"), P("tm", "panel", None))
    return jax.shard_map(
        per_device,
        mesh=mesh,
        in_specs=placed,
        out_specs=(P("tm", "panel"), P("tm", "panel", None)),
        check_vma=False,
    )
```

```python
import jax
import jax.numpy as jnp
from jax import lax
from jax.experimental import pallas as pl
from jax.experimental.pallas import tpu as pltpu
from jax.sharding import PartitionSpec as P

D = 512
ROWS = 64
HALF = 256
AUG = D + 8
NN = (((1,), (0,)), ((), ()))
NT = (((1,), (1,)), ((), ()))
VMEM = pl.BlockSpec(memory_space=pltpu.VMEM)
ANY = pl.BlockSpec(memory_space=pl.ANY)
F32 = jnp.float32
BF16 = jnp.bfloat16


def full(*dims):
    return jax.ShapeDtypeStruct(dims, F32)


def part(*dims):
    return jax.ShapeDtypeStruct(dims, BF16)


def split(a):
    high = a.astype(BF16)
    return high, (a - high.astype(F32)).astype(BF16)


def dot(a, b, dims):
    return lax.dot_general(a, b, dims, preferred_element_type=F32)


def dot3(a, b, dims):
    return dot(a[0], b[0], dims) + (dot(a[0], b[1], dims) + dot(a[1], b[0], dims))


def call(kernel, name, outs, args, scratch=(), us=0, mib=18, outside=()):
    return pl.pallas_call(
        kernel,
        out_shape=outs,
        in_specs=[ANY if index in outside else VMEM for index in range(len(args))],
        out_specs=[VMEM] * len(outs),
        scratch_shapes=list(scratch),
        compiler_params=pltpu.CompilerParams(vmem_limit_bytes=mib << 20),
        cost_estimate=pl.CostEstimate(
            flops=us * 10**9, bytes_accessed=0, transcendentals=0
        ),
        name=name,
    )(*args)


def gate(value, *others):
    return pl.pallas_call(
        lambda *refs: None,
        out_shape=jax.ShapeDtypeStruct(value.shape, value.dtype),
        in_specs=[ANY] * (1 + len(others)),
        out_specs=ANY,
        input_output_aliases={0: 0},
        compiler_params=pltpu.CompilerParams(vmem_limit_bytes=1 << 20),
        name="gate",
    )(value, *others)


def position():
    panel, block = lax.axis_index("panel"), lax.axis_index("tm")
    return panel // 2, panel % 2, block % 4


def own_rows(size=ROWS):
    return pl.ds(pl.multiple_of(lax.axis_index("panel") * size, size), size)


def places(mine, c):
    toward = 1 - 2 * c
    own = [mine, mine - toward, mine + toward, mine + 2]
    other = [mine, mine + toward, mine - toward, mine + 2]
    return [((place + 4) % 4, c) for place in own] + [((place + 4) % 4, 1 - c) for place in other]


def panels(z, c):
    return [2 * place + core for place, core in places(z, c)]


def chip_pieces(refs, z, c):
    pair, near, other, far, far_other = refs
    size, toward = far.shape[0], 1 - 2 * c
    pieces = [
        (ref, core * size, 2 * (place % 4) + core)
        for ref, place in ((pair, z), (near, z - toward + 4), (other, z + toward + 4))
        for core in range(2)
    ]
    return pieces + [(far, 0, 2 * ((z + 2) % 4) + c), (far_other, 0, 2 * ((z + 2) % 4) + 1 - c)]


def at(panel, size=ROWS):
    return pl.ds(pl.multiple_of(panel * size, size), size)


def block_kernel(*refs):
    pieces, (e_hi, e_lo), suffix, (total, mine, sem) = refs[:8], refs[8:10], refs[10:18], refs[18:]
    z, c, _ = position()
    copy = pltpu.make_async_copy(pieces[0], mine, sem)
    copy.start()
    spots = list(zip((mine, *pieces[1:]), panels(z, c)))
    for index, (piece, panel) in enumerate(spots[1:] + spots[:1]):
        if index == 7:
            copy.wait()
        for k in range(4):
            high, low = split(piece[k * ROWS : (k + 1) * ROWS, :])
            to_hi, to_lo = (e_hi.at[k], e_lo.at[k]) if k < 3 else suffix[6:8]
            to_hi[at(panel), :] = high
            to_lo[at(panel), :] = low
    for k in (2, 1, 0):
        product = dot3((e_hi[k], e_lo[k]), (suffix[2 * k + 2][...], suffix[2 * k + 3][...]), NN)
        suffix[2 * k][...], suffix[2 * k + 1][...] = split(product)
    total[...] = product


def pack_kernel(noise, offsets, packed, sem):
    copy = pltpu.make_async_copy(noise, packed.at[:HALF], sem)
    copy.start()
    packed[HALF:, :] = jnp.zeros((8, D), F32)
    for panel in range(8):

        @pl.when(lax.axis_index("panel") == panel)
        def _():
            packed[HALF : HALF + 4, panel * ROWS : (panel + 1) * ROWS] = offsets[...]

    copy.wait()


def pair_kernel(mine, other, pair):
    c = position()[1]
    rows = mine.shape[0]
    pair[at(c, rows), :] = mine[...]
    pair[at(1 - c, rows), :] = other[...]


def cut_kernel(pair, mine):
    rows = mine.shape[0]
    mine[...] = pair[at(position()[1], rows), :]


def congruence(gain, cov, scratch):
    scratch[:D, :] = dot3(gain, split(cov[:D, :]), NN)
    scratch[D:, :] = cov[D:, :]
    return dot3(split(scratch[...]), gain, NT)


def noise_kernel(e_hi, e_lo, *refs):
    pieces, (rows_out, means_out, whole, scratch) = refs[:5], refs[5:]
    z, c, _ = position()
    size, pieces = HALF + 8, chip_pieces(pieces, z, c)
    offsets = sum(ref[start + HALF : start + size, :] for ref, start, _ in pieces)
    row = lax.broadcasted_iota(jnp.int32, (8, D), 0)
    means_out[...] = jnp.zeros((8, D), F32)
    for k in (3, 2, 1, 0):
        if k == 3:
            whole[...] = jnp.zeros((AUG, D), F32)
        else:
            whole[...] = congruence((e_hi[k], e_lo[k]), whole[...], scratch)
        for ref, start, panel in pieces:
            whole[at(panel), :] += ref[start + k * ROWS : start + (k + 1) * ROWS, :]
        offset = jnp.sum(jnp.where(row == k, offsets, 0.0), axis=0, keepdims=True)
        whole[D:, :] += jnp.where(row == 0, offset, 0.0)
        rows_out[k] = whole[own_rows(), :]
        means_out[k : k + 1, :] = whole[D : D + 1, :]


def gather_gains(own_hi, own_lo, near, other, far, far_other, a_hi, a_lo):
    _, c, y = position()
    toward, across = 1 - 2 * c, (y + 2) % 4
    a_hi[y] = own_hi[...]
    a_lo[y] = own_lo[...]
    a_hi[(y - toward + 4) % 4], a_lo[(y - toward + 4) % 4] = split(near[...])
    a_hi[(y + toward + 4) % 4], a_lo[(y + toward + 4) % 4] = split(other[...])
    a_hi[across, at(c, HALF), :], a_lo[across, at(c, HALF), :] = split(far[...])
    a_hi[across, at(1 - c, HALF), :], a_lo[across, at(1 - c, HALF), :] = split(far_other[...])


def eye_parts():
    same = lax.broadcasted_iota(jnp.int32, (D, D), 0) == lax.broadcasted_iota(jnp.int32, (D, D), 1)
    return jnp.where(same, 1.0, 0.0).astype(BF16), jnp.zeros((D, D), BF16)


def rows_congruence(left, right, cov, scratch):
    scratch[:ROWS, :] = dot3(left, split(cov[:D, :]), NN)
    scratch[ROWS:, :] = cov[D:, :]
    return dot3(split(scratch[...]), right, NT)


def prefix_kernel(cov, moved, *refs):
    blocks, (gain, to_third, to_second, to_first, a_hi, a_lo, f_hi, f_lo, short) = refs[:6], refs[6:]
    y = position()[2]
    gather_gains(*blocks, a_hi, a_lo)

    @pl.when(y == 0)
    def _():
        f_hi[...], f_lo[...] = eye_parts()

    head = (a_hi[0], a_lo[0])
    for block in (1, 2, 3):

        @pl.when(y == block)
        def _():
            f_hi[...], f_lo[...] = head

        if block < 3:
            head = split(dot3(head, (a_hi[block], a_lo[block]), NN))
    term = rows_congruence(
        (f_hi[own_rows(), :], f_lo[own_rows(), :]), (f_hi[...], f_lo[...]), cov[...], short
    )
    for message in (to_third, to_second, to_first):
        message[: ROWS + 8, :] = term
    for message, whole in ((to_first, cov), (to_second, moved)):
        message[ROWS + 8 : 2 * ROWS + 8, :] = whole[own_rows(), :]
        message[2 * ROWS + 8 :, :] = whole[D:, :]
    twice = (y + 2) % 4
    to_third[ROWS + 8 :, :] = rows_congruence(
        (a_hi[twice, own_rows(), :], a_lo[twice, own_rows(), :]), (a_hi[twice], a_lo[twice]), moved[...], short
    )
    f_hi[...], f_lo[...] = head
    half = at(position()[1], HALF)
    gain[...] = dot3((f_hi[half, :], f_lo[half, :]), (a_hi[3], a_lo[3]), NN)


def second_kernel(cov, near, other, moved, a_hi, a_lo, scratch):
    _, c, _ = position()
    for core, piece in enumerate((near, other)):

        @pl.when(c == core)
        def _():
            a_hi[...], a_lo[...] = split(piece[...])

    moved[...] = congruence((a_hi[...], a_lo[...]), cov[...], scratch)


def sum_kernel(own, third, second, first, total, beyond):
    y, size = position()[2], ROWS + 8
    total[...] = own[:size, :] + third[:size, :] + second[:size, :] + first[:size, :]
    beyond[...] = (
        jnp.where(y < 1, third[size:, :], 0.0)
        + jnp.where(y < 2, second[size:, :], 0.0)
        + jnp.where(y < 3, first[size:, :], 0.0)
    )


def tail_kernel(*refs):
    blocks, (p_hi, p_lo, a_hi, a_lo) = refs[:6], refs[6:]
    y = position()[2]
    gather_gains(*blocks, a_hi, a_lo)

    @pl.when(y == 3)
    def _():
        p_hi[...], p_lo[...] = eye_parts()

    tail = (a_hi[3], a_lo[3])
    for block in (2, 1, 0):

        @pl.when(y == block)
        def _():
            p_hi[...], p_lo[...] = tail

        if block > 0:
            tail = split(dot3((a_hi[block], a_lo[block]), tail, NN))


def blocks_kernel(first, second, third, fourth, rows, back, ahead, across):
    z, x = position()[0], lax.axis_index("tm") // 4
    for index, piece in enumerate((first, second, third, fourth)):
        known = x + index < 3 if index < 3 else x >= 0
        rows[index * ROWS : (index + 1) * ROWS, :] = jnp.where(known, piece[:ROWS, :], 0.0)
    for step, messages in ((0, (back, ahead, across)), (1, (back,)), (2, (back,)), (3, (ahead,))):
        block = rows[:, at((z + step) % 4, 128)]
        for message in messages:
            column = 128 if message is ahead and step else 128 * step
            message[:, column : column + 128] = block


def fill_symmetric(cov, index, own, back, ahead, across, z, c):
    rows = slice(index * ROWS, (index + 1) * ROWS)
    a, b, far = (z + 1) % 4, (z + 3) % 4, (z + 2) % 4
    for half in range(2):
        core = c if half == 0 else 1 - c

        def place(row, column, value):
            start = pl.multiple_of(row * 128 + core * ROWS, ROWS)
            cov[pl.ds(start, ROWS), at(column, 128)] = value

        cov[pl.ds(pl.multiple_of(z * 128 + core * ROWS, ROWS), ROWS), :] = own[half][rows, :]
        place(a, a, back[half][rows, :128])
        place(a, far, back[half][rows, 128:256])
        place(a, b, back[half][rows, 256:])
        place(b, b, ahead[half][rows, :128])
        place(b, far, ahead[half][rows, 128:])
        place(far, far, across[half][rows, :])
    for row, column in ((z, a), (z, b), (z, far), (a, far), (a, b), (b, far)):
        cov[at(column, 128), at(row, 128)] = cov[at(row, 128), at(column, 128)].T


def outer_kernel(p_hi, p_lo, *refs):
    suffix, pieces, (b_hi, b_lo, x_hi, x_lo, s_hi, s_lo, gain) = refs[:8], refs[8:10], refs[10:]
    c = position()[1]
    for core, piece in zip((c, 1 - c), pieces):
        gain[at(core, HALF), :] = piece[...]
    for k in range(4):
        s_hi[k * ROWS : (k + 1) * ROWS, :] = suffix[2 * k][own_rows(), :]
        s_lo[k * ROWS : (k + 1) * ROWS, :] = suffix[2 * k + 1][own_rows(), :]
    b_hi[0], b_lo[0] = p_hi[...], p_lo[...]
    x_hi[0], x_lo[0] = split(dot3((s_hi[...], s_lo[...]), (b_hi[0], b_lo[0]), NN))
    parts = split(gain[...])
    b_hi[1], b_lo[1] = split(dot3((b_hi[0], b_lo[0]), parts, NN))
    x_hi[1], x_lo[1] = split(dot3((x_hi[0], x_lo[0]), parts, NN))


def outermost_kernel(b_hi, b_lo, x_hi, x_lo, mine, other, c_hi, c_lo, y_hi, y_lo, gain):
    c = position()[1]
    for core, piece in zip((c, 1 - c), (mine, other)):
        gain[at(core, HALF), :] = piece[...]
    parts = split(gain[...])
    c_hi[...], c_lo[...] = split(dot3((b_hi[1], b_lo[1]), parts, NN))
    y_hi[...], y_lo[...] = split(dot3((x_hi[1], x_lo[1]), parts, NN))


def final_kernel(b_hi, b_lo, x_hi, x_lo, c_hi, c_lo, y_hi, y_lo, s_hi, s_lo, rows_in, means_in, *refs):
    suffix, offsets, pieces, (out, means, cov, stack, short, every) = refs[:8], refs[8:12], refs[12:20], refs[20:]
    z, c, _ = position()
    inner = 0.0
    for index in range(4):
        fill_symmetric(cov, index, pieces[0:2], pieces[2:4], pieces[4:6], pieces[6:8], z, c)
        if index < 2:
            left, right = (x_hi[index], x_lo[index]), (b_hi[index], b_lo[index])
        elif index == 2:
            left, right = (y_hi[...], y_lo[...]), (c_hi[...], c_lo[...])
        else:
            left = (s_hi[...], s_lo[...])
        stack[:HALF, :] = dot3(left, split(cov[...]), NN)
        known = lax.axis_index("tm") // 4 + index < 3 if index < 3 else z >= 0
        stack[HALF:, :] = jnp.where(known, offsets[index][ROWS:, :], 0.0)
        if index < 3:
            inner = inner + dot3(split(stack[...]), right, NT)
    stack[...] = stack[...] + inner
    for k in range(4):
        short[:ROWS, :] = stack[k * ROWS : (k + 1) * ROWS, :]
        short[ROWS:, :] = stack[HALF:, :]
        result = dot3(split(short[...]), (suffix[2 * k][...], suffix[2 * k + 1][...]), NT)
        out[k] = result[:ROWS, :] + rows_in[k]
        every[k : k + 1, :] = result[ROWS : ROWS + 1, :] + means_in[k : k + 1, :]
    for panel in range(8):

        @pl.when(lax.axis_index("panel") == panel)
        def _():
            means[...] = every[:4, panel * ROWS : (panel + 1) * ROWS]


def per_device(transitions, offsets, noise_cov):
    def other_core(value):
        return lax.ppermute(value, "panel", [(2 * z + c, 2 * z + 1 - c) for z in range(4) for c in range(2)])

    def along_y(value, step):
        return lax.ppermute(
            value, "tm", [(4 * x + y, 4 * x + (y + step) % 4) for x in range(4) for y in range(4)]
        )

    def back_x(value, step):
        return lax.ppermute(
            value, "tm", [(4 * x + y, 4 * ((x - step) % 4) + y) for x in range(4) for y in range(4)]
        )

    def along_z(value, step):
        return lax.ppermute(
            value, "panel", [(2 * z + c, 2 * ((z + step) % 4) + c) for z in range(4) for c in range(2)]
        )

    def paired_z(value, step):
        return lax.ppermute(
            value, "panel", [(2 * z + c, 2 * ((z + step * (1 - 2 * c)) % 4) + c) for z in range(4) for c in range(2)]
        )

    def paired_y(value, step):
        pairs = []
        for x in range(4):
            for y in range(4):
                for panel in range(8):
                    to = 4 * x + (y + step * (1 - 2 * (panel % 2))) % 4
                    pairs.append((8 * (4 * x + y) + panel, 8 * to + panel))
        return lax.ppermute(value, ("tm", "panel"), pairs)

    def exchange(value, paired):
        first = paired(value, 1)
        return [first, paired(value, -1), paired(first, 1)]

    def both_cores(pieces):
        return pieces + [other_core(piece) for piece in pieces]

    def whole_z(value):
        return both_cores([value] + exchange(value, paired_z))

    (noise,) = call(
        pack_kernel,
        "pack",
        [full(HALF + 8, D)],
        [noise_cov.reshape(HALF, D), offsets],
        [pltpu.SemaphoreType.DMA],
        outside=(0,),
    )
    other_noise = other_core(noise)
    own = transitions.reshape(HALF, D)
    first, second, third = exchange(own, paired_z)
    (pair,) = call(pair_kernel, "pair", [full(2 * HALF + 16, D)], [gate(noise, second), other_noise])
    steps = both_cores([own, first, second, gate(third, pair)])
    e_hi, e_lo, *rest = call(
        block_kernel,
        "block",
        [part(3, D, D)] * 2 + [part(D, D)] * 8 + [full(D, D)],
        steps,
        [pltpu.VMEM((HALF, D), F32), pltpu.SemaphoreType.DMA],
        outside=(0,),
    )
    suffix, total = rest[:8], rest[8]
    near_gain, near_noise = paired_y(total, 1), paired_z(pair, 1)
    (half_gain,) = call(cut_kernel, "cut", [full(HALF, D)], [near_gain])
    (half_noise,) = call(cut_kernel, "cut", [full(HALF + 8, D)], [near_noise])
    far_gain, far_noise = paired_y(half_gain, 1), gate(paired_z(half_noise, 1), half_gain)
    other_gain = other_core(near_gain)
    other_far = other_core(far_noise)
    rows, means, cov = call(
        noise_kernel,
        "noise",
        [full(4, ROWS, D), full(8, D), full(AUG, D)],
        [e_hi, e_lo, pair, near_noise, other_core(near_noise), far_noise, other_far],
        [pltpu.VMEM((AUG, D), F32)],
    )
    (moved,) = call(
        second_kernel,
        "second",
        [full(AUG, D)],
        [cov, near_gain, other_gain],
        [pltpu.VMEM((D, D), BF16), pltpu.VMEM((D, D), BF16), pltpu.VMEM((AUG, D), F32)],
    )
    far_gain = gate(far_gain, moved)
    blocks = [suffix[0], suffix[1], near_gain, other_gain, far_gain, other_core(far_gain)]
    gain, to_third, to_second, to_first = call(
        prefix_kernel,
        "prefix",
        [full(HALF, D)] + [full(2 * ROWS + 16, D)] * 3,
        [cov, moved, *blocks],
        [pltpu.VMEM((4, D, D), BF16)] * 2 + [pltpu.VMEM((D, D), BF16)] * 2 + [pltpu.VMEM((ROWS + 8, D), F32)],
    )
    from_third, from_second, from_first = along_y(to_third, 1), along_y(to_second, 2), along_y(to_first, 3)
    p_hi, p_lo = call(
        tail_kernel,
        "tail",
        [part(D, D)] * 2,
        blocks,
        [pltpu.VMEM((4, D, D), BF16)] * 2,
    )
    next_gain = back_x(gain, 1)
    total, beyond = call(
        sum_kernel,
        "sum",
        [full(ROWS + 8, D)] * 2,
        [gate(to_third, next_gain, p_hi), from_third, from_second, from_first],
    )
    next_gain = gate(next_gain, total)
    far_covs = [back_x(total, step) for step in (1, 2, 3)]
    own, *messages = call(
        blocks_kernel,
        "blocks",
        [full(4 * ROWS, D), full(4 * ROWS, 384), full(4 * ROWS, 256), full(4 * ROWS, 128)],
        [*far_covs, beyond],
    )
    back, ahead, across = (along_z(value, step) for value, step in zip(messages, (-1, 1, 2)))
    after_gain = back_x(gate(next_gain, far_covs[0], far_covs[1], far_covs[2]), 1)
    b_hi, b_lo, x_hi, x_lo, s_hi, s_lo = call(
        outer_kernel,
        "outer",
        [part(2, D, D), part(2, D, D), part(2, HALF, D), part(2, HALF, D), part(HALF, D), part(HALF, D)],
        [p_hi, p_lo, *suffix, next_gain, other_core(next_gain)],
        [pltpu.VMEM((D, D), F32)],
    )
    after_gain = gate(after_gain, back, ahead, across, s_hi)
    outermost = call(
        outermost_kernel,
        "outermost",
        [part(D, D), part(D, D), part(HALF, D), part(HALF, D)],
        [b_hi, b_lo, x_hi, x_lo, after_gain, other_core(after_gain)],
        [pltpu.VMEM((D, D), F32)],
    )
    covs = [own, back, ahead, across]
    covs = [piece for value in covs for piece in (value, other_core(value))]
    out, mean_rows = call(
        final_kernel,
        "final",
        [full(4, ROWS, D), full(4, ROWS)],
        [b_hi, b_lo, x_hi, x_lo, *outermost, s_hi, s_lo, rows, means, *suffix, *far_covs, beyond, *covs],
        [
            pltpu.VMEM((D, D), F32),
            pltpu.VMEM((HALF + 8, D), F32),
            pltpu.VMEM((ROWS + 8, D), F32),
            pltpu.VMEM((8, D), F32),
        ],
        mib=24,
    )
    return mean_rows, out


def solution(mesh):
    placed = (P("tm", "panel", None), P("tm", "panel"), P("tm", "panel", None))
    return jax.shard_map(
        per_device,
        mesh=mesh,
        in_specs=placed,
        out_specs=(P("tm", "panel"), P("tm", "panel", None)),
        check_vma=False,
    )
```

```python
import jax
import jax.numpy as jnp
from jax import lax
from jax.experimental import pallas as pl
from jax.experimental.pallas import tpu as pltpu
from jax.sharding import PartitionSpec as P

D = 512
ROWS = 64
HALF = 256
AUG = D + 8
NN = (((1,), (0,)), ((), ()))
NT = (((1,), (1,)), ((), ()))
VMEM = pl.BlockSpec(memory_space=pltpu.VMEM)
ANY = pl.BlockSpec(memory_space=pl.ANY)
F32 = jnp.float32
BF16 = jnp.bfloat16


def full(*dims):
    return jax.ShapeDtypeStruct(dims, F32)


def part(*dims):
    return jax.ShapeDtypeStruct(dims, BF16)


def split(a):
    high = a.astype(BF16)
    return high, (a - high.astype(F32)).astype(BF16)


def dot(a, b, dims):
    return lax.dot_general(a, b, dims, preferred_element_type=F32)


def dot3(a, b, dims):
    return dot(a[0], b[0], dims) + (dot(a[0], b[1], dims) + dot(a[1], b[0], dims))


def call(kernel, name, outs, args, scratch=(), us=0, mib=18, outside=()):
    return pl.pallas_call(
        kernel,
        out_shape=outs,
        in_specs=[ANY if index in outside else VMEM for index in range(len(args))],
        out_specs=[VMEM] * len(outs),
        scratch_shapes=list(scratch),
        compiler_params=pltpu.CompilerParams(vmem_limit_bytes=mib << 20),
        cost_estimate=pl.CostEstimate(
            flops=us * 10**9, bytes_accessed=0, transcendentals=0
        ),
        name=name,
    )(*args)


def gate(value, *others):
    return pl.pallas_call(
        lambda *refs: None,
        out_shape=jax.ShapeDtypeStruct(value.shape, value.dtype),
        in_specs=[ANY] * (1 + len(others)),
        out_specs=ANY,
        input_output_aliases={0: 0},
        compiler_params=pltpu.CompilerParams(vmem_limit_bytes=1 << 20),
        name="gate",
    )(value, *others)


def position():
    panel, block = lax.axis_index("panel"), lax.axis_index("tm")
    return panel // 2, panel % 2, block % 4


def own_rows(size=ROWS):
    return pl.ds(pl.multiple_of(lax.axis_index("panel") * size, size), size)


def places(mine, c):
    toward = 1 - 2 * c
    own = [mine, mine - toward, mine + toward, mine + 2]
    other = [mine, mine + toward, mine - toward, mine + 2]
    return [((place + 4) % 4, c) for place in own] + [((place + 4) % 4, 1 - c) for place in other]


def panels(z, c):
    return [2 * place + core for place, core in places(z, c)]


def chip_pieces(refs, z, c):
    pair, near, other, far, far_other = refs
    size, toward = far.shape[0], 1 - 2 * c
    pieces = [
        (ref, core * size, 2 * (place % 4) + core)
        for ref, place in ((pair, z), (near, z - toward + 4), (other, z + toward + 4))
        for core in range(2)
    ]
    return pieces + [(far, 0, 2 * ((z + 2) % 4) + c), (far_other, 0, 2 * ((z + 2) % 4) + 1 - c)]


def at(panel, size=ROWS):
    return pl.ds(pl.multiple_of(panel * size, size), size)


def block_kernel(*refs):
    pieces, (e_hi, e_lo), suffix, (total, mine, sem) = refs[:8], refs[8:10], refs[10:18], refs[18:]
    z, c, _ = position()
    copy = pltpu.make_async_copy(pieces[0], mine, sem)
    copy.start()
    spots = list(zip((mine, *pieces[1:]), panels(z, c)))
    for index, (piece, panel) in enumerate(spots[1:] + spots[:1]):
        if index == 7:
            copy.wait()
        for k in range(4):
            high, low = split(piece[k * ROWS : (k + 1) * ROWS, :])
            to_hi, to_lo = (e_hi.at[k], e_lo.at[k]) if k < 3 else suffix[6:8]
            to_hi[at(panel), :] = high
            to_lo[at(panel), :] = low
    for k in (2, 1, 0):
        product = dot3((e_hi[k], e_lo[k]), (suffix[2 * k + 2][...], suffix[2 * k + 3][...]), NN)
        suffix[2 * k][...], suffix[2 * k + 1][...] = split(product)
    total[...] = product


def pack_kernel(noise, offsets, packed, sem):
    copy = pltpu.make_async_copy(noise, packed.at[:HALF], sem)
    copy.start()
    packed[HALF:, :] = jnp.zeros((8, D), F32)
    for panel in range(8):

        @pl.when(lax.axis_index("panel") == panel)
        def _():
            packed[HALF : HALF + 4, panel * ROWS : (panel + 1) * ROWS] = offsets[...]

    copy.wait()


def pair_kernel(mine, other, pair):
    c = position()[1]
    rows = mine.shape[0]
    pair[at(c, rows), :] = mine[...]
    pair[at(1 - c, rows), :] = other[...]


def cut_kernel(pair, mine):
    rows = mine.shape[0]
    mine[...] = pair[at(position()[1], rows), :]


def congruence(gain, cov, scratch):
    scratch[:D, :] = dot3(gain, split(cov[:D, :]), NN)
    scratch[D:, :] = cov[D:, :]
    return dot3(split(scratch[...]), gain, NT)


def noise_kernel(e_hi, e_lo, *refs):
    pieces, (rows_out, means_out, whole, scratch) = refs[:5], refs[5:]
    z, c, _ = position()
    size, pieces = HALF + 8, chip_pieces(pieces, z, c)
    offsets = sum(ref[start + HALF : start + size, :] for ref, start, _ in pieces)
    row = lax.broadcasted_iota(jnp.int32, (8, D), 0)
    means_out[...] = jnp.zeros((8, D), F32)
    for k in (3, 2, 1, 0):
        if k == 3:
            whole[...] = jnp.zeros((AUG, D), F32)
        else:
            whole[...] = congruence((e_hi[k], e_lo[k]), whole[...], scratch)
        for ref, start, panel in pieces:
            whole[at(panel), :] += ref[start + k * ROWS : start + (k + 1) * ROWS, :]
        offset = jnp.sum(jnp.where(row == k, offsets, 0.0), axis=0, keepdims=True)
        whole[D:, :] += jnp.where(row == 0, offset, 0.0)
        rows_out[k] = whole[own_rows(), :]
        means_out[k : k + 1, :] = whole[D : D + 1, :]


def gather_gains(own_hi, own_lo, near, other, far, far_other, a_hi, a_lo):
    _, c, y = position()
    toward, across = 1 - 2 * c, (y + 2) % 4
    a_hi[y] = own_hi[...]
    a_lo[y] = own_lo[...]
    a_hi[(y - toward + 4) % 4], a_lo[(y - toward + 4) % 4] = split(near[...])
    a_hi[(y + toward + 4) % 4], a_lo[(y + toward + 4) % 4] = split(other[...])
    a_hi[across, at(c, HALF), :], a_lo[across, at(c, HALF), :] = split(far[...])
    a_hi[across, at(1 - c, HALF), :], a_lo[across, at(1 - c, HALF), :] = split(far_other[...])


def eye_parts():
    same = lax.broadcasted_iota(jnp.int32, (D, D), 0) == lax.broadcasted_iota(jnp.int32, (D, D), 1)
    return jnp.where(same, 1.0, 0.0).astype(BF16), jnp.zeros((D, D), BF16)


def rows_congruence(left, right, cov, scratch):
    scratch[:ROWS, :] = dot3(left, split(cov[:D, :]), NN)
    scratch[ROWS:, :] = cov[D:, :]
    return dot3(split(scratch[...]), right, NT)


def prefix_kernel(cov, moved, *refs):
    blocks, (gain, to_third, to_second, to_first, a_hi, a_lo, f_hi, f_lo, short) = refs[:6], refs[6:]
    y = position()[2]
    gather_gains(*blocks, a_hi, a_lo)

    @pl.when(y == 0)
    def _():
        f_hi[...], f_lo[...] = eye_parts()

    head = (a_hi[0], a_lo[0])
    for block in (1, 2, 3):

        @pl.when(y == block)
        def _():
            f_hi[...], f_lo[...] = head

        if block < 3:
            head = split(dot3(head, (a_hi[block], a_lo[block]), NN))
    term = rows_congruence(
        (f_hi[own_rows(), :], f_lo[own_rows(), :]), (f_hi[...], f_lo[...]), cov[...], short
    )
    for message in (to_third, to_second, to_first):
        message[: ROWS + 8, :] = term
    for message, whole in ((to_first, cov), (to_second, moved)):
        message[ROWS + 8 : 2 * ROWS + 8, :] = whole[own_rows(), :]
        message[2 * ROWS + 8 :, :] = whole[D:, :]
    twice = (y + 2) % 4
    to_third[ROWS + 8 :, :] = rows_congruence(
        (a_hi[twice, own_rows(), :], a_lo[twice, own_rows(), :]), (a_hi[twice], a_lo[twice]), moved[...], short
    )
    f_hi[...], f_lo[...] = head
    half = at(position()[1], HALF)
    gain[...] = dot3((f_hi[half, :], f_lo[half, :]), (a_hi[3], a_lo[3]), NN)


def second_kernel(cov, near, other, moved, a_hi, a_lo, scratch):
    _, c, _ = position()
    for core, piece in enumerate((near, other)):

        @pl.when(c == core)
        def _():
            a_hi[...], a_lo[...] = split(piece[...])

    moved[...] = congruence((a_hi[...], a_lo[...]), cov[...], scratch)


def sum_kernel(own, third, second, first, total, beyond):
    y, size = position()[2], ROWS + 8
    total[...] = own[:size, :] + third[:size, :] + second[:size, :] + first[:size, :]
    beyond[...] = (
        jnp.where(y < 1, third[size:, :], 0.0)
        + jnp.where(y < 2, second[size:, :], 0.0)
        + jnp.where(y < 3, first[size:, :], 0.0)
    )


def tail_kernel(*refs):
    blocks, (p_hi, p_lo, a_hi, a_lo) = refs[:6], refs[6:]
    y = position()[2]
    gather_gains(*blocks, a_hi, a_lo)

    @pl.when(y == 3)
    def _():
        p_hi[...], p_lo[...] = eye_parts()

    tail = (a_hi[3], a_lo[3])
    for block in (2, 1, 0):

        @pl.when(y == block)
        def _():
            p_hi[...], p_lo[...] = tail

        if block > 0:
            tail = split(dot3((a_hi[block], a_lo[block]), tail, NN))


def blocks_kernel(first, second, third, fourth, rows, back, ahead, across):
    z, x = position()[0], lax.axis_index("tm") // 4
    for index, piece in enumerate((first, second, third, fourth)):
        known = x + index < 3 if index < 3 else x >= 0
        rows[index * ROWS : (index + 1) * ROWS, :] = jnp.where(known, piece[:ROWS, :], 0.0)
    for step, messages in ((0, (back, ahead, across)), (1, (back,)), (2, (back,)), (3, (ahead,))):
        block = rows[:, at((z + step) % 4, 128)]
        for message in messages:
            column = 128 if message is ahead and step else 128 * step
            message[:, column : column + 128] = block


def fill_symmetric(cov, index, own, back, ahead, across, z, c):
    rows = slice(index * ROWS, (index + 1) * ROWS)
    a, b, far = (z + 1) % 4, (z + 3) % 4, (z + 2) % 4
    for half in range(2):
        core = c if half == 0 else 1 - c

        def place(row, column, value):
            start = pl.multiple_of(row * 128 + core * ROWS, ROWS)
            cov[pl.ds(start, ROWS), at(column, 128)] = value

        cov[pl.ds(pl.multiple_of(z * 128 + core * ROWS, ROWS), ROWS), :] = own[half][rows, :]
        place(a, a, back[half][rows, :128])
        place(a, far, back[half][rows, 128:256])
        place(a, b, back[half][rows, 256:])
        place(b, b, ahead[half][rows, :128])
        place(b, far, ahead[half][rows, 128:])
        place(far, far, across[half][rows, :])
    for row, column in ((z, a), (z, b), (z, far), (a, far), (a, b), (b, far)):
        cov[at(column, 128), at(row, 128)] = cov[at(row, 128), at(column, 128)].T


def outer_kernel(p_hi, p_lo, *refs):
    suffix, pieces, (b_hi, b_lo, x_hi, x_lo, s_hi, s_lo, gain) = refs[:8], refs[8:10], refs[10:]
    c = position()[1]
    for core, piece in zip((c, 1 - c), pieces):
        gain[at(core, HALF), :] = piece[...]
    for k in range(4):
        s_hi[k * ROWS : (k + 1) * ROWS, :] = suffix[2 * k][own_rows(), :]
        s_lo[k * ROWS : (k + 1) * ROWS, :] = suffix[2 * k + 1][own_rows(), :]
    b_hi[0], b_lo[0] = p_hi[...], p_lo[...]
    x_hi[0], x_lo[0] = split(dot3((s_hi[...], s_lo[...]), (b_hi[0], b_lo[0]), NN))
    parts = split(gain[...])
    b_hi[1], b_lo[1] = split(dot3((b_hi[0], b_lo[0]), parts, NN))
    x_hi[1], x_lo[1] = split(dot3((x_hi[0], x_lo[0]), parts, NN))


def outermost_kernel(b_hi, b_lo, x_hi, x_lo, mine, other, c_hi, c_lo, y_hi, y_lo, gain):
    c = position()[1]
    for core, piece in zip((c, 1 - c), (mine, other)):
        gain[at(core, HALF), :] = piece[...]
    parts = split(gain[...])
    c_hi[...], c_lo[...] = split(dot3((b_hi[1], b_lo[1]), parts, NN))
    y_hi[...], y_lo[...] = split(dot3((x_hi[1], x_lo[1]), parts, NN))


def final_kernel(b_hi, b_lo, x_hi, x_lo, c_hi, c_lo, y_hi, y_lo, s_hi, s_lo, rows_in, means_in, *refs):
    suffix, offsets, pieces, (out, means, cov, stack, short, every) = refs[:8], refs[8:12], refs[12:20], refs[20:]
    z, c, _ = position()
    inner = 0.0
    for index in range(4):
        fill_symmetric(cov, index, pieces[0:2], pieces[2:4], pieces[4:6], pieces[6:8], z, c)
        if index < 2:
            left, right = (x_hi[index], x_lo[index]), (b_hi[index], b_lo[index])
        elif index == 2:
            left, right = (y_hi[...], y_lo[...]), (c_hi[...], c_lo[...])
        else:
            left = (s_hi[...], s_lo[...])
        stack[:HALF, :] = dot3(left, split(cov[...]), NN)
        known = lax.axis_index("tm") // 4 + index < 3 if index < 3 else z >= 0
        stack[HALF:, :] = jnp.where(known, offsets[index][ROWS:, :], 0.0)
        if index < 3:
            inner = inner + dot3(split(stack[...]), right, NT)
    stack[...] = stack[...] + inner
    for k in range(4):
        short[:ROWS, :] = stack[k * ROWS : (k + 1) * ROWS, :]
        short[ROWS:, :] = stack[HALF:, :]
        result = dot3(split(short[...]), (suffix[2 * k][...], suffix[2 * k + 1][...]), NT)
        out[k] = result[:ROWS, :] + rows_in[k]
        every[k : k + 1, :] = result[ROWS : ROWS + 1, :] + means_in[k : k + 1, :]
    for panel in range(8):

        @pl.when(lax.axis_index("panel") == panel)
        def _():
            means[...] = every[:4, panel * ROWS : (panel + 1) * ROWS]


def per_device(transitions, offsets, noise_cov):
    def other_core(value):
        return lax.ppermute(value, "panel", [(2 * z + c, 2 * z + 1 - c) for z in range(4) for c in range(2)])

    def along_y(value, step):
        return lax.ppermute(
            value, "tm", [(4 * x + y, 4 * x + (y + step) % 4) for x in range(4) for y in range(4)]
        )

    def back_x(value, step):
        return lax.ppermute(
            value, "tm", [(4 * x + y, 4 * ((x - step) % 4) + y) for x in range(4) for y in range(4)]
        )

    def along_z(value, step):
        return lax.ppermute(
            value, "panel", [(2 * z + c, 2 * ((z + step) % 4) + c) for z in range(4) for c in range(2)]
        )

    def paired_z(value, step):
        return lax.ppermute(
            value, "panel", [(2 * z + c, 2 * ((z + step * (1 - 2 * c)) % 4) + c) for z in range(4) for c in range(2)]
        )

    def paired_y(value, step):
        pairs = []
        for x in range(4):
            for y in range(4):
                for panel in range(8):
                    to = 4 * x + (y + step * (1 - 2 * (panel % 2))) % 4
                    pairs.append((8 * (4 * x + y) + panel, 8 * to + panel))
        return lax.ppermute(value, ("tm", "panel"), pairs)

    def exchange(value, paired):
        first = paired(value, 1)
        return [first, paired(value, -1), paired(first, 1)]

    def both_cores(pieces):
        return pieces + [other_core(piece) for piece in pieces]

    def whole_z(value):
        return both_cores([value] + exchange(value, paired_z))

    (noise,) = call(
        pack_kernel,
        "pack",
        [full(HALF + 8, D)],
        [noise_cov.reshape(HALF, D), offsets],
        [pltpu.SemaphoreType.DMA],
        outside=(0,),
    )
    other_noise = other_core(noise)
    own = transitions.reshape(HALF, D)
    first, second, third = exchange(own, paired_z)
    (pair,) = call(pair_kernel, "pair", [full(2 * HALF + 16, D)], [gate(noise, second), other_noise])
    steps = both_cores([own, first, second, gate(third, pair)])
    e_hi, e_lo, *rest = call(
        block_kernel,
        "block",
        [part(3, D, D)] * 2 + [part(D, D)] * 8 + [full(D, D)],
        steps,
        [pltpu.VMEM((HALF, D), F32), pltpu.SemaphoreType.DMA],
        outside=(0,),
    )
    suffix, total = rest[:8], rest[8]
    near_gain, near_noise = paired_y(total, 1), paired_z(pair, 1)
    (half_gain,) = call(cut_kernel, "cut", [full(HALF, D)], [near_gain])
    (half_noise,) = call(cut_kernel, "cut", [full(HALF + 8, D)], [near_noise])
    far_gain, far_noise = paired_y(half_gain, 1), gate(paired_z(half_noise, 1), half_gain)
    other_gain = other_core(near_gain)
    other_far = other_core(far_noise)
    rows, means, cov = call(
        noise_kernel,
        "noise",
        [full(4, ROWS, D), full(8, D), full(AUG, D)],
        [e_hi, e_lo, pair, near_noise, other_core(near_noise), far_noise, other_far],
        [pltpu.VMEM((AUG, D), F32)],
    )
    (moved,) = call(
        second_kernel,
        "second",
        [full(AUG, D)],
        [cov, near_gain, other_gain],
        [pltpu.VMEM((D, D), BF16), pltpu.VMEM((D, D), BF16), pltpu.VMEM((AUG, D), F32)],
    )
    far_gain = gate(far_gain, moved)
    blocks = [suffix[0], suffix[1], near_gain, other_gain, far_gain, other_core(far_gain)]
    gain, to_third, to_second, to_first = call(
        prefix_kernel,
        "prefix",
        [full(HALF, D)] + [full(2 * ROWS + 16, D)] * 3,
        [cov, moved, *blocks],
        [pltpu.VMEM((4, D, D), BF16)] * 2 + [pltpu.VMEM((D, D), BF16)] * 2 + [pltpu.VMEM((ROWS + 8, D), F32)],
    )
    from_third, from_second, from_first = along_y(to_third, 1), along_y(to_second, 2), along_y(to_first, 3)
    p_hi, p_lo = call(
        tail_kernel,
        "tail",
        [part(D, D)] * 2,
        blocks,
        [pltpu.VMEM((4, D, D), BF16)] * 2,
    )
    next_gain = back_x(gain, 1)
    total, beyond = call(
        sum_kernel,
        "sum",
        [full(ROWS + 8, D)] * 2,
        [gate(to_third, next_gain, p_hi), from_third, from_second, from_first],
    )
    next_gain = gate(next_gain, total)
    far_covs = [back_x(total, step) for step in (1, 2, 3)]
    own, *messages = call(
        blocks_kernel,
        "blocks",
        [full(4 * ROWS, D), full(4 * ROWS, 384), full(4 * ROWS, 256), full(4 * ROWS, 128)],
        [*far_covs, beyond],
    )
    back, ahead, across = (along_z(value, step) for value, step in zip(messages, (-1, 1, 2)))
    after_gain = back_x(gate(next_gain, far_covs[0], far_covs[1]), 1)
    b_hi, b_lo, x_hi, x_lo, s_hi, s_lo = call(
        outer_kernel,
        "outer",
        [part(2, D, D), part(2, D, D), part(2, HALF, D), part(2, HALF, D), part(HALF, D), part(HALF, D)],
        [p_hi, p_lo, *suffix, next_gain, other_core(next_gain)],
        [pltpu.VMEM((D, D), F32)],
    )
    after_gain = gate(after_gain, back, ahead, across, s_hi)
    outermost = call(
        outermost_kernel,
        "outermost",
        [part(D, D), part(D, D), part(HALF, D), part(HALF, D)],
        [b_hi, b_lo, x_hi, x_lo, after_gain, other_core(after_gain)],
        [pltpu.VMEM((D, D), F32)],
    )
    covs = [own, back, ahead, across]
    covs = [piece for value in covs for piece in (value, other_core(value))]
    out, mean_rows = call(
        final_kernel,
        "final",
        [full(4, ROWS, D), full(4, ROWS)],
        [b_hi, b_lo, x_hi, x_lo, *outermost, s_hi, s_lo, rows, means, *suffix, *far_covs, beyond, *covs],
        [
            pltpu.VMEM((D, D), F32),
            pltpu.VMEM((HALF + 8, D), F32),
            pltpu.VMEM((ROWS + 8, D), F32),
            pltpu.VMEM((8, D), F32),
        ],
        mib=24,
    )
    return mean_rows, out


def solution(mesh):
    placed = (P("tm", "panel", None), P("tm", "panel"), P("tm", "panel", None))
    return jax.shard_map(
        per_device,
        mesh=mesh,
        in_specs=placed,
        out_specs=(P("tm", "panel"), P("tm", "panel", None)),
        check_vma=False,
    )
```
